1024 devices in a mesh: grp: 32 (over x, y), peer: 32 (over z, core).
Axes of the slice: x: 4, y: 8, z: 16, core: 2. Of those that a mesh axis runs over, the one named last changes fastest.
Arguments:
- labels: bfloat16 [1048576, 256], P(('grp', 'peer')), may hold values from -6 to 6
- node_degree: int32 [1048576], P(('grp', 'peer')), may hold values from 1 to 64
- edge_degree: int32 [524288], P(('grp', 'peer')), may hold values from 1 to 64
- labeled_mask: int32 [1048576], P(('grp', 'peer')), may hold values 0 or 1
- seed_labels: int32 [1048576], P(('grp', 'peer')), may hold values from 0 to 255
- local_incidence: bfloat16 [1048576, 512], P(('grp', 'peer')), may hold values from -0.25 to 0.25
- tiles: bfloat16 [1024, 64, 32, 16], P(('grp', 'peer')), may hold values from -1.5 to 1.5
- out_block: int32 [1024, 64], P(('grp', 'peer')), may hold values from 0 to 31
- out_count: int32 [1024, 64], P(('grp', 'peer')), may hold values 0 or 1
- in_edge: int32 [1024, 64], P(('grp', 'peer')), may hold values from 0 to 31
Outputs:
- spread_labels: bfloat16 [1048576, 256], P(('grp', 'peer'))
The draws below stay inside these ranges and needn't reach their ends.
All inputs are finite; a program needn't handle non-finite values. No bound on the sum of `labeled_mask` or of `out_count` on one device may be relied on, other than what follows from the above.
Results may differ from the reference program's by a relative error of at most 0.008.
Values may be sent and summed in bfloat16 or wider, within the bound.
A program may use at most 32 MiB of HBM per device.

```python
import jax
import jax.numpy as jnp
from jax import lax

C = 256
BLK = 32
EW = 16
ROUNDS = 2
ROWS_DEV = 1024
EDGE_DEV = 512
SLOTS = 64
NODES = 1048576
EDGES = 524288
N_GRP = 32
N_PEER = 32


def set_ends(values, rng, least, high):
    extent = values.shape
    place = [jax.random.randint(jax.random.fold_in(rng, axis), (), 0, extent[axis]) for axis in range(len(extent))]
    values = values.at[tuple(place)].set(least)
    longest = extent.index(max(extent))
    place[longest] = (place[longest] + 1) % extent[longest]
    return values.at[tuple(place)].set(high)


def block_levels(own_key, shape, shards, low, high):
    level, own = 1.0, jax.random.fold_in(own_key, 6)
    for axis_at, parts in shards:
        steps = jnp.exp(jax.random.uniform(jax.random.fold_in(own, axis_at), (parts,), jnp.float32, low / len(shards), high / len(shards)))
        level = level * jnp.repeat(steps, shape[axis_at] // parts).reshape([-1 if axis == axis_at else 1 for axis in range(len(shape))])
    return level


def normal_values(rng, shape, scale, bound, cuts=(), kind=jnp.bfloat16):
    loudness = block_levels(rng, shape, cuts, -0.22, 0.18) if cuts else 1.0
    result = jax.random.normal(rng, shape, jnp.float32) * scale * loudness
    return jnp.minimum(jnp.maximum(result, -bound), bound).astype(kind)


def setup_inputs(seed: int = 0) -> dict:
    streams_of = jax.random.split(jax.random.key(seed), 11)
    return {
        "labels": normal_values(streams_of[0], (NODES, C), 1.0, 6.0, ((0, 1024),)),
        "node_degree": set_ends(jax.random.randint(streams_of[1], (NODES,), 1, 65), jax.random.fold_in(streams_of[1], 1), 1, 64).astype(jnp.int32),
        "edge_degree": set_ends(jax.random.randint(streams_of[2], (EDGES,), 1, 65), jax.random.fold_in(streams_of[2], 1), 1, 64).astype(jnp.int32),
        "labeled_mask": set_ends((jax.random.randint(streams_of[3], (NODES,), 0, 8) < 1).astype(jnp.int32), jax.random.fold_in(streams_of[3], 1), 0, 1),
        "seed_labels": set_ends(jax.random.randint(streams_of[4], (NODES,), 0, C), jax.random.fold_in(streams_of[4], 1), 0, C - 1).astype(jnp.int32),
        "local_incidence": normal_values(streams_of[5], (NODES, EDGE_DEV), EDGE_DEV ** -0.5, 0.25, ((0, 1024),)),
        "tiles": normal_values(streams_of[6], (N_GRP * N_PEER, SLOTS, BLK, EW), EW ** -0.5, 1.5, ((0, 1024),)),
        "out_block": set_ends(jax.random.randint(streams_of[7], (N_GRP * N_PEER, SLOTS), 0, ROWS_DEV // BLK), jax.random.fold_in(streams_of[7], 1), 0, (ROWS_DEV // BLK) - 1).astype(jnp.int32),
        "out_count": set_ends((jax.random.randint(streams_of[8], (N_GRP * N_PEER, SLOTS), 0, 4) < 3).astype(jnp.int32), jax.random.fold_in(streams_of[8], 1), 0, 1),
        "in_edge": set_ends(jax.random.randint(streams_of[9], (N_GRP * N_PEER, SLOTS), 0, EDGE_DEV // EW), jax.random.fold_in(streams_of[9], 1), 0, (EDGE_DEV // EW) - 1).astype(jnp.int32),
    }


eps = 1e-05

def partners(device):
    group_index = device // N_PEER
    member = device % N_PEER
    slot_index = jnp.arange(N_PEER + N_GRP, dtype=jnp.int32)
    is_peer = slot_index < N_PEER
    other_member = jnp.where(is_peer, slot_index, member)
    other_group = jnp.where(is_peer, group_index, slot_index - N_PEER)
    partner = (other_group * N_PEER + other_member).astype(jnp.int32)
    facing = jnp.where(is_peer, member, N_PEER + group_index).astype(jnp.int32)
    return (partner, facing)

def reference(labels, node_degree, edge_degree, labeled_mask, seed_labels, local_incidence, tiles, out_block, out_count, in_edge):
    devices = N_GRP * N_PEER
    n_blocks = ROWS_DEV // BLK
    e_blocks = EDGE_DEV // EW
    incidence = local_incidence.reshape(devices, ROWS_DEV, EDGE_DEV)
    node_scale = lax.rsqrt(node_degree.astype(jnp.float32)).reshape(devices, ROWS_DEV, 1)
    edge_div = edge_degree.astype(jnp.float32).reshape(devices, EDGE_DEV, 1)
    live_slots = out_count.astype(jnp.float32)
    seed_rows = jnp.sqrt(jnp.float32(C)) * (seed_labels[:, None] == jnp.arange(C, dtype=jnp.int32)[None, :]).astype(jnp.float32)
    seed_rows = seed_rows.reshape(devices, ROWS_DEV, C)
    labeled = (labeled_mask == 1).reshape(devices, ROWS_DEV, 1)
    current = labels
    for round_index in range(ROUNDS):
        scaled = (current.astype(jnp.float32).reshape(devices, ROWS_DEV, C) * node_scale).astype(jnp.bfloat16)
        blocks_all = scaled.reshape(devices, n_blocks, BLK, C)

        def edge_side(device):
            partner, facing = partners(device)
            source = blocks_all[partner, out_block[partner, facing]]
            weights = tiles[partner, facing]
            slot_terms = jnp.einsum('sbw,sbc->swc', weights.astype(jnp.float32), source.astype(jnp.float32), precision=lax.Precision.HIGHEST)
            slot_terms = slot_terms * live_slots[partner, facing][:, None, None]
            choose = (in_edge[device][:, None] == jnp.arange(e_blocks, dtype=jnp.int32)[None, :]).astype(jnp.float32)
            remote = jnp.einsum('se,swc->ewc', choose, slot_terms, precision=lax.Precision.HIGHEST).reshape(EDGE_DEV, C)
            local_part = lax.dot_general(incidence[device], scaled[device], (((0,), (0,)), ((), ())), preferred_element_type=jnp.float32)
            return ((local_part + remote) / edge_div[device]).astype(jnp.bfloat16)
        aggregate = lax.map(edge_side, jnp.arange(devices, dtype=jnp.int32))
        agg_blocks = aggregate.reshape(devices, e_blocks, EW, C)

        def node_side(device):
            partner, facing = partners(device)
            chosen = agg_blocks[partner, in_edge[partner, facing]]
            slot_terms = jnp.einsum('sbw,swc->sbc', tiles[device].astype(jnp.float32), chosen.astype(jnp.float32), precision=lax.Precision.HIGHEST)
            slot_terms = slot_terms * live_slots[device][:, None, None]
            choose = (out_block[device][:, None] == jnp.arange(n_blocks, dtype=jnp.int32)[None, :]).astype(jnp.float32)
            remote = jnp.einsum('sn,sbc->nbc', choose, slot_terms, precision=lax.Precision.HIGHEST).reshape(ROWS_DEV, C)
            local_part = jnp.dot(incidence[device], aggregate[device], preferred_element_type=jnp.float32)
            node_total = local_part + remote
            mean_square = lax.optimization_barrier(jnp.mean(node_total * node_total, axis=-1, keepdims=True))
            normed = node_total * lax.rsqrt(mean_square + eps)
            return jnp.where(labeled[device], seed_rows[device], normed).astype(jnp.bfloat16)
        current = lax.map(node_side, jnp.arange(devices, dtype=jnp.int32)).reshape(devices * ROWS_DEV, C)
    return current
```

```python
import functools

import jax
import jax.numpy as jnp
from jax import lax
from jax.experimental import pallas as pl
from jax.experimental.pallas import tpu as pltpu
from jax.sharding import PartitionSpec as P

ROUNDS = 2
PARTS = 2
CHUNK = 16
LANES = 128
EPS = 1e-05
MESH = pl.DeviceIdType.MESH
F32 = jnp.float32
BF16 = jnp.bfloat16


def iota(shape, dim):
    return lax.broadcasted_iota(jnp.int32, shape, dim)


def dot(a, b):
    return jnp.dot(a, b, preferred_element_type=F32)


def dot_t(a, b):
    return lax.dot_general(a, b, (((1,), (1,)), ((), ())), preferred_element_type=F32)


def tiled(a, count):
    return a if count == 1 else jnp.concatenate([a] * count, axis=1)


def loop(count, body):
    def step(i, carry):
        body(i)
        return carry

    lax.fori_loop(0, count, step, 0)


def rows_of(i, count):
    return pl.ds(pl.multiple_of(i * count, count), count)


def kernel(
    sizes,
    labels_hbm,
    tiles_hbm,
    inc_hbm,
    node_hbm,
    edge_hbm,
    mask_hbm,
    seed_hbm,
    block_hbm,
    count_hbm,
    in_hbm,
    out_ref,
    labels,
    tiles,
    inc,
    node_ref,
    edge_ref,
    mask_ref,
    seed_ref,
    block_ref,
    count_ref,
    in_ref,
    out_buf,
    inc_t,
    spread,
    spread_t,
    choose,
    choose_t,
    tile_col,
    block_col,
    scale_col,
    seed_col,
    div_col,
    scaled,
    agg,
    edge_sum,
    node_sum,
    fsend,
    frecv,
    bsend,
    brecv,
    in_sem,
    out_sem,
    ready,
    fsend_sem,
    frecv_sem,
    bsend_sem,
    brecv_sem,
):
    n, slots, block, width, rows, edges, classes, chunk = sizes
    cols = classes // PARTS
    n_chunks = slots // chunk
    crows = chunk * width
    flat = slots * width
    fold = LANES // block
    g, p = lax.axis_index("grp"), lax.axis_index("peer")

    with jax.named_scope("greet"):
        moves = (
            (node_hbm, node_ref),
            (labels_hbm, labels),
            (tiles_hbm, tiles),
            (block_hbm, block_ref),
            (count_hbm, count_ref),
            (in_hbm, in_ref),
            (edge_hbm, edge_ref),
            (mask_hbm, mask_ref),
            (seed_hbm, seed_ref),
            (inc_hbm, inc),
        )
        loads = [pltpu.make_async_copy(src, dst, in_sem.at[k]) for k, (src, dst) in enumerate(moves)]
        for load in loads:
            load.start()

        barrier = pltpu.get_barrier_semaphore()

        def greet(j):
            @pl.when(j > p)
            def _():
                pl.semaphore_signal(barrier, inc=1, device_id=(g, j), device_id_type=MESH)

            @pl.when(j > g)
            def _():
                pl.semaphore_signal(barrier, inc=1, device_id=(j, p), device_id_type=MESH)

        loop(n, greet)

        @pl.when(p + g > 0)
        def _():
            pl.semaphore_wait(barrier, p + g)

        def answer(j):
            @pl.when(j < p)
            def _():
                pl.semaphore_signal(ready.at[p], inc=1, device_id=(g, j), device_id_type=MESH)

            @pl.when(j < g)
            def _():
                pl.semaphore_signal(ready.at[n + g], inc=1, device_id=(j, p), device_id_type=MESH)

        loop(n, answer)

    def column(ref):
        k, lanes = ref.shape
        pick = (iota((k, k * LANES), 1) // LANES == iota((k, k * LANES), 0)).astype(BF16)
        wide = lax.dot_general(ref[...].astype(F32).astype(BF16), pick, (((0,), (0,)), ((), ())), preferred_element_type=F32)
        return [wide[:, i * LANES : (i + 1) * LANES] for i in range(k)]

    with jax.named_scope("scale"):
        loads[0].wait()
        for i, part in enumerate(column(node_ref)):
            scale_col[i * LANES : (i + 1) * LANES, :] = lax.rsqrt(part)
        loads[1].wait()

        def scale_rows(i):
            at = rows_of(i, LANES)
            scaled[at, :] = (labels[at, :].astype(F32) * tiled(scale_col[at, :], classes // LANES)).astype(BF16)

        loop(rows // LANES, scale_rows)

    def pick_rows(i, value):
        slot = i * (LANES // width) + iota((LANES, slots), 0) // width
        return jnp.where(slot == iota((LANES, slots), 1), value, 0.0).astype(BF16)

    def slot_col(i, ref):
        return dot_t(pick_rows(i, 1.0), jnp.broadcast_to(ref[...].astype(F32), (LANES, slots)).astype(BF16))

    with jax.named_scope("tiles"):
        for load in loads[2:6]:
            load.wait()
        gather = (iota((block * width, LANES), 0) // width == iota((block * width, LANES), 1) % block).astype(BF16)

        def first_product(i):
            at = rows_of(i, LANES)
            wide = dot_t(pick_rows(i, count_ref[...].astype(F32)), tiles[...])
            same = iota((LANES, block * width), 0) % width == iota((LANES, block * width), 1) % width
            weight = dot(jnp.where(same, wide, 0.0).astype(BF16), gather)
            place = slot_col(i, block_ref)
            tile_col[at, :] = weight
            block_col[at, :] = place
            lane_block = (iota((LANES, LANES), 1) // block).astype(F32)
            parts = []
            for k in range(rows // LANES):
                piece = jnp.where(place == lane_block + float(k * fold), weight, 0.0).astype(BF16)
                spread_t[at, k * LANES : (k + 1) * LANES] = piece
                parts.append(piece)
            product = dot(jnp.concatenate(parts, axis=1), scaled[...]).astype(BF16)
            for h in range(PARTS):
                fsend[0, h, at, :] = product[:, h * cols : (h + 1) * cols]

        loop(flat // LANES, first_product)

    def copy_to(r, h, kind, other, src, dst, send_sem, recv_sem):
        me = g if kind else p
        pltpu.make_async_remote_copy(
            src_ref=src.at[r, h, rows_of(kind * n + other, width)],
            dst_ref=dst.at[r, h, rows_of(kind * n + me, width)],
            send_sem=send_sem.at[r, h],
            recv_sem=recv_sem.at[r, h, (kind * n + me) // chunk],
            device_id=(other, p) if kind else (g, other),
            device_id_type=MESH,
        ).start()

    def around(j, me):
        half = (j + 1) // 2
        return (me + n // 2 + half * (1 - 2 * (j % 2))) % n

    def send_all(r, h, *way):
        def one(j):
            copy_to(r, h, 0, around(j, p), *way)
            copy_to(r, h, 1, around(j, g), *way)

        loop(n - 1, one)

    def keep(r, h, src, dst, send_sem, recv_sem):
        for slot in (p, n + g):
            at = rows_of(slot, width)
            pltpu.make_async_copy(src.at[r, h, at], dst.at[r, h, at], recv_sem.at[r, h, slot // chunk]).start()

    def arrive(r, h, c, dst, recv_sem):
        part = dst.at[r, h, pl.ds(c * crows, crows)]
        pltpu.make_async_copy(part, part, recv_sem.at[r, h, c]).wait()

    out_way = (fsend, frecv, fsend_sem, frecv_sem)
    back_way = (bsend, brecv, bsend_sem, brecv_sem)

    with jax.named_scope("first_send"):

        def early(j):
            @pl.when(j < p)
            def _():
                copy_to(0, 0, 0, jnp.where(j % 2 == 0, j // 2, p - 1 - j // 2), *out_way)

            other = jnp.where(j < g, j, j + 1)

            @pl.when(j >= g)
            def _():
                pl.semaphore_wait(ready.at[n + other], 1)

            copy_to(0, 0, 1, other, *out_way)

        loop(n - 1, early)

        def late(j):
            @pl.when(j >= p)
            def _():
                pl.semaphore_wait(ready.at[j + 1], 1)
                copy_to(0, 0, 0, j + 1, *out_way)

        loop(n - 1, late)
        keep(0, 0, *out_way)
        for h in range(1, PARTS):
            send_all(0, h, *out_way)
            keep(0, h, *out_way)

    for r in range(ROUNDS):
        if r > 0:
            with jax.named_scope("out_send"):

                def product_rows(i):
                    at = rows_of(i, crows)
                    product = dot(spread_t[at, :], scaled[...]).astype(BF16)
                    for h in range(PARTS):
                        fsend[r, h, at, :] = product[:, h * cols : (h + 1) * cols]

                loop(n_chunks, product_rows)
                for h in range(PARTS):
                    send_all(r, h, *out_way)
                    keep(r, h, *out_way)
        else:
            with jax.named_scope("build"):
                for load in loads[6:]:
                    load.wait()

                for i, part in enumerate(column(edge_ref)):
                    div_col[i * LANES : (i + 1) * LANES, :] = part
                known, class_of = column(mask_ref), column(seed_ref)
                for i in range(rows // LANES):
                    seed_col[i * LANES : (i + 1) * LANES, :] = jnp.where(known[i] == 1.0, class_of[i], -1.0)

                for i in range(rows // LANES):
                    at = slice(i * LANES, (i + 1) * LANES)
                    inc_t[:, at] = inc[at, :].astype(F32).T.astype(BF16)

                for i in range(flat // LANES):
                    at = slice(i * LANES, (i + 1) * LANES)
                    row = (iota((LANES, LANES), 0) % width).astype(F32)
                    target = slot_col(i, in_ref) * float(width) + row
                    target_t = target.T
                    for k in range(edges // LANES):
                        e = slice(k * LANES, (k + 1) * LANES)
                        lane = (iota((LANES, LANES), 1) + k * LANES).astype(F32)
                        choose_t[at, e] = jnp.where(target == lane, 1.0, 0.0).astype(BF16)
                        down = (iota((LANES, LANES), 0) + k * LANES).astype(F32)
                        choose[e, at] = jnp.where(target_t == down, 1.0, 0.0).astype(BF16)
                    weight, place = tile_col[at, :].T, block_col[at, :].T
                    down_block = (iota((LANES, LANES), 0) // block).astype(F32)
                    for k in range(rows // LANES):
                        b = slice(k * LANES, (k + 1) * LANES)
                        spread[b, at] = jnp.where(place == down_block + float(k * fold), weight, 0.0).astype(BF16)

        with jax.named_scope("local_edge"):

            def local_edge(i):
                at = rows_of(i, 256)
                edge_sum[at, :] = dot(inc_t[at, :], scaled[...])

            loop(edges // 256, local_edge)

        for h in range(PARTS):
            part = slice(h * cols, (h + 1) * cols)
            with jax.named_scope("edge_wait"):
                for c in range(n_chunks):
                    arrive(r, h, c, frecv, frecv_sem)
            with jax.named_scope("edge"):

                def remote_edge(i):
                    at = rows_of(i, 256)
                    total = edge_sum[at, part] + dot(choose[at, :], frecv[r, h])
                    agg[at, part] = (total / tiled(div_col[at, :], cols // LANES)).astype(BF16)

                loop(edges // 256, remote_edge)
            with jax.named_scope("back_send"):

                def chosen(i):
                    at = rows_of(i, crows)
                    bsend[r, h, at, :] = dot(choose_t[at, :], agg[:, part]).astype(BF16)

                loop(n_chunks, chosen)
                send_all(r, h, *back_way)
                keep(r, h, *back_way)
            with jax.named_scope("local_node"):

                def local_node(i):
                    at = rows_of(i, 256)
                    node_sum[at, part] = dot(inc[at, :], agg[:, part])

                loop(rows // 256, local_node)

        for h in range(PARTS):
            part = slice(h * cols, (h + 1) * cols)
            with jax.named_scope("node_wait"):
                for c in range(n_chunks):
                    arrive(r, h, c, brecv, brecv_sem)
            if h == PARTS - 1:
                break
            with jax.named_scope("node"):

                def remote_node(i):
                    at = rows_of(i, 256)
                    node_sum[at, part] = node_sum[at, part] + dot(spread[at, :], brecv[r, h])

                loop(rows // 256, remote_node)

        with jax.named_scope("finish"):

            def finish(i):
                at = rows_of(i, LANES)
                last = dot(spread[at, :], brecv[r, PARTS - 1])
                total = node_sum[at, :]
                if PARTS > 1:
                    total = jnp.concatenate([total[:, : classes - cols], total[:, classes - cols :] + last], axis=1)
                else:
                    total = total + last
                mean_square = jnp.sum(total * total, axis=-1, keepdims=True) * (1.0 / classes)
                normed = total * lax.rsqrt(mean_square + EPS)
                known = tiled(seed_col[at, :], classes // LANES)
                seeds = jnp.where(iota((LANES, classes), 1).astype(F32) == known, float(classes) ** 0.5, 0.0)
                current = jnp.where(known >= 0.0, seeds, normed).astype(BF16)
                if r < ROUNDS - 1:
                    scaled[at, :] = (current.astype(F32) * tiled(scale_col[at, :], classes // LANES)).astype(BF16)
                else:
                    out_buf[at, :] = current

            loop(rows // LANES, finish)

    with jax.named_scope("store"):
        store = pltpu.make_async_copy(out_buf, out_ref, out_sem)
        store.start()
        for r in range(ROUNDS):
            for h in range(PARTS):
                for buf, sem in ((fsend, fsend_sem), (bsend, bsend_sem)):
                    sent = buf.at[r, h, pl.ds(0, (slots - 2) * width)]
                    pltpu.make_async_copy(sent, sent, sem.at[r, h]).wait()
        store.wait()


def local(labels, node_degree, edge_degree, labeled_mask, seed_labels, local_incidence, tiles, out_block, out_count, in_edge):
    n = lax.axis_size("peer")
    rows, classes = labels.shape
    edges = local_incidence.shape[1]
    _, slots, block, width = tiles.shape
    chunk = min(CHUNK, n)
    flat = slots * width
    sizes = (n, slots, block, width, rows, edges, classes, chunk)
    travel = (ROUNDS, PARTS, flat, classes // PARTS)
    hbm = pl.BlockSpec(memory_space=pltpu.HBM)
    dma = pltpu.SemaphoreType.DMA
    args = (
        labels,
        tiles[0].transpose(1, 2, 0).reshape(block * width, slots),
        local_incidence,
        node_degree.reshape(rows // LANES, LANES),
        edge_degree.reshape(edges // LANES, LANES),
        labeled_mask.reshape(rows // LANES, LANES),
        seed_labels.reshape(rows // LANES, LANES),
        out_block,
        out_count,
        in_edge,
    )
    return pl.pallas_call(
        functools.partial(kernel, sizes),
        out_shape=jax.ShapeDtypeStruct((rows, classes), BF16),
        in_specs=[hbm] * len(args),
        out_specs=pl.BlockSpec(memory_space=pl.ANY),
        scratch_shapes=[pltpu.VMEM(a.shape, a.dtype) for a in args]
        + [
            pltpu.VMEM((rows, classes), BF16),
            pltpu.VMEM((edges, rows), BF16),
            pltpu.VMEM((rows, flat), BF16),
            pltpu.VMEM((flat, rows), BF16),
            pltpu.VMEM((edges, flat), BF16),
            pltpu.VMEM((flat, edges), BF16),
            pltpu.VMEM((flat, LANES), F32),
            pltpu.VMEM((flat, LANES), F32),
            pltpu.VMEM((rows, LANES), F32),
            pltpu.VMEM((rows, LANES), F32),
            pltpu.VMEM((edges, LANES), F32),
            pltpu.VMEM((rows, classes), BF16),
            pltpu.VMEM((edges, classes), BF16),
            pltpu.VMEM((edges, classes), F32),
            pltpu.VMEM((rows, classes), F32),
            pltpu.VMEM(travel, BF16),
            pltpu.VMEM(travel, BF16),
            pltpu.VMEM(travel, BF16),
            pltpu.VMEM(travel, BF16),
            dma((len(args),)),
            dma,
            pltpu.SemaphoreType.REGULAR((slots,)),
            dma((ROUNDS, PARTS)),
            dma((ROUNDS, PARTS, slots // chunk)),
            dma((ROUNDS, PARTS)),
            dma((ROUNDS, PARTS, slots // chunk)),
        ],
        compiler_params=pltpu.CompilerParams(collective_id=0, has_side_effects=True, vmem_limit_bytes=60 << 20),
    )(*args)


def solution(mesh):
    split = ("grp", "peer")
    specs = (
        P(split, None),
        P(split),
        P(split),
        P(split),
        P(split),
        P(split, None),
        P(split, None, None, None),
        P(split, None),
        P(split, None),
        P(split, None),
    )
    return jax.shard_map(local, mesh=mesh, in_specs=specs, out_specs=P(split, None), check_vma=False)
```

```python
import functools

import jax
import jax.numpy as jnp
from jax import lax
from jax.experimental import pallas as pl
from jax.experimental.pallas import tpu as pltpu
from jax.sharding import PartitionSpec as P

ROUNDS = 2
PARTS = 2
LANES = 128
EPS = 1e-05
MESH = pl.DeviceIdType.MESH
F32 = jnp.float32
BF16 = jnp.bfloat16


def iota(shape, dim):
    return lax.broadcasted_iota(jnp.int32, shape, dim)


def dot(a, b):
    return jnp.dot(a, b, preferred_element_type=F32)


def dot_t(a, b):
    return lax.dot_general(a, b, (((1,), (1,)), ((), ())), preferred_element_type=F32)


def tiled(a, count):
    return a if count == 1 else jnp.concatenate([a] * count, axis=1)


def span(first, end, body):
    def step(i, carry):
        body(i)
        return carry

    lax.fori_loop(first, end, step, 0)


def loop(count, body):
    span(0, count, body)


def rows_of(i, count):
    return pl.ds(pl.multiple_of(i * count, count), count)


def kernel(
    sizes,
    labels_hbm,
    tiles_hbm,
    inc_hbm,
    node_hbm,
    edge_hbm,
    mask_hbm,
    seed_hbm,
    block_hbm,
    count_hbm,
    in_hbm,
    out_ref,
    labels,
    tiles,
    inc,
    node_ref,
    edge_ref,
    mask_ref,
    seed_ref,
    block_ref,
    count_ref,
    in_ref,
    inc_t,
    spread,
    spread_t,
    choose,
    choose_t,
    tile_col,
    block_col,
    scale_col,
    seed_col,
    div_col,
    scaled,
    agg,
    edge_sum,
    node_sum,
    fsend,
    frecv,
    bsend,
    brecv,
    in_sem,
    ready,
    fsend_sem,
    frecv_sem,
    bsend_sem,
    brecv_sem,
):
    n, slots, block, width, rows, edges, classes = sizes
    cols = classes // PARTS
    flat = slots * width
    half = flat // 2
    fold = LANES // block
    g, p = lax.axis_index("grp"), lax.axis_index("peer")

    with jax.named_scope("greet"):
        moves = (
            (node_hbm, node_ref),
            (labels_hbm, labels),
            (tiles_hbm, tiles),
            (block_hbm, block_ref),
            (count_hbm, count_ref),
            (in_hbm, in_ref),
            (edge_hbm, edge_ref),
            (mask_hbm, mask_ref),
            (seed_hbm, seed_ref),
            (inc_hbm, inc),
        )
        loads = [pltpu.make_async_copy(src, dst, in_sem.at[k]) for k, (src, dst) in enumerate(moves)]
        for load in loads:
            load.start()

        barrier = pltpu.get_barrier_semaphore()

        def call(j, kind):
            where = (j, p) if kind else (g, j)
            pl.semaphore_signal(barrier, inc=1, device_id=where, device_id_type=MESH)

        def answer(j, kind):
            where = (j, p) if kind else (g, j)
            pl.semaphore_signal(ready.at[n + g if kind else p], inc=1, device_id=where, device_id_type=MESH)

        span(p + 1, n, lambda j: call(j, 0))
        span(g + 1, n, lambda j: call(j, 1))

        @pl.when(p + g > 0)
        def _():
            pl.semaphore_wait(barrier, p + g)

        span(0, p, lambda j: answer(j, 0))
        span(0, g, lambda j: answer(j, 1))

    def column(ref):
        k, lanes = ref.shape
        pick = (iota((k, k * LANES), 1) // LANES == iota((k, k * LANES), 0)).astype(BF16)
        wide = lax.dot_general(ref[...].astype(F32).astype(BF16), pick, (((0,), (0,)), ((), ())), preferred_element_type=F32)
        return [wide[:, i * LANES : (i + 1) * LANES] for i in range(k)]

    with jax.named_scope("scale"):
        loads[0].wait()
        for i, part in enumerate(column(node_ref)):
            scale_col[i * LANES : (i + 1) * LANES, :] = lax.rsqrt(part)
        loads[1].wait()

        for i in range(rows // LANES):
            at = slice(i * LANES, (i + 1) * LANES)
            scaled[at, :] = (labels[at, :].astype(F32) * tiled(scale_col[at, :], classes // LANES)).astype(BF16)

    def pick_rows(first, count, value):
        slot = first + iota((count, slots), 0) // width
        return jnp.where(slot == iota((count, slots), 1), value, 0.0).astype(BF16)

    def slot_col(first, count, ref):
        values = jnp.broadcast_to(ref[...].astype(F32), (LANES, slots)).astype(BF16)
        return dot_t(pick_rows(first, count, 1.0), values)

    def first_product(kind):
        at = slice(kind * half, (kind + 1) * half)
        wide = dot_t(pick_rows(kind * n, half, count_ref[...].astype(F32)), tiles[...])
        same = iota((half, block * width), 0) % width == iota((half, block * width), 1) % width
        gather = (iota((block * width, LANES), 0) // width == iota((block * width, LANES), 1) % block).astype(BF16)
        weight = dot(jnp.where(same, wide, 0.0).astype(BF16), gather)
        place = slot_col(kind * n, half, block_ref)
        tile_col[at, :] = weight
        block_col[at, :] = place
        lane_block = (iota((half, LANES), 1) // block).astype(F32)
        for k in range(rows // LANES):
            piece = jnp.where(place == lane_block + float(k * fold), weight, 0.0)
            spread_t[at, k * LANES : (k + 1) * LANES] = piece.astype(BF16)
        out_product(0, kind)

    def out_product(r, kind):
        at = slice(kind * half, (kind + 1) * half)
        product = dot(spread_t[at, :], scaled[...]).astype(BF16)
        for h in range(PARTS):
            fsend[r, h, at, :] = product[:, h * cols : (h + 1) * cols]

    def copy_to(r, h, kind, other, src, dst, send_sem, recv_sem):
        me = g if kind else p
        pltpu.make_async_remote_copy(
            src_ref=src.at[r, h, rows_of(kind * n + other, width)],
            dst_ref=dst.at[r, h, rows_of(kind * n + me, width)],
            send_sem=send_sem.at[r, h],
            recv_sem=recv_sem.at[r, h, kind],
            device_id=(other, p) if kind else (g, other),
            device_id_type=MESH,
        ).start()

    def around(me, send):
        def wrap(x):
            return jnp.where(x >= n, x - n, x)

        def both(t):
            send(wrap(me + (n // 2) - t))
            send(wrap(me + (n // 2) + t))

        send(wrap(me + n // 2))
        span(1, n // 2, both)

    def keep(r, h, kind, src, dst, send_sem, recv_sem):
        at = rows_of(n + g if kind else p, width)
        pltpu.make_async_copy(src.at[r, h, at], dst.at[r, h, at], recv_sem.at[r, h, kind]).start()

    def send_all(r, h, kind, *way):
        around(g if kind else p, lambda other: copy_to(r, h, kind, other, *way))
        keep(r, h, kind, *way)

    def arrive(r, h, kind, dst, recv_sem):
        part = dst.at[r, h, pl.ds(kind * half, half)]
        pltpu.make_async_copy(part, part, recv_sem.at[r, h, kind]).wait()

    out_way = (fsend, frecv, fsend_sem, frecv_sem)
    back_way = (bsend, brecv, bsend_sem, brecv_sem)

    with jax.named_scope("first_send"):
        for load in loads[2:5]:
            load.wait()
        first_product(0)

        def early(other, h):
            @pl.when(other < p)
            def _():
                copy_to(0, h, 0, other, *out_way)

        def late(other, h):
            if h == 0:
                pl.semaphore_wait(ready.at[other], 1)
            copy_to(0, h, 0, other, *out_way)

        def latest(other, h):
            @pl.when(jnp.logical_and(other > p, other >= n // 2))
            def _():
                late(other, h)

        def across(j, h):
            if h == 0:
                pl.semaphore_wait(ready.at[n + j], 1)
            copy_to(0, h, 1, j, *out_way)

        around(p, lambda other: early(other, 0))
        first_product(1)
        span(0, g, lambda j: copy_to(0, 0, 1, j, *out_way))
        span(g + 1, n, lambda j: across(j, 0))
        for h in range(1, PARTS):
            around(p, lambda other: early(other, h))
        span(p + 1, n // 2, lambda j: late(j, 0))
        around(p, lambda other: latest(other, 0))
        keep(0, 0, 0, *out_way)
        keep(0, 0, 1, *out_way)
        for h in range(1, PARTS):
            span(p + 1, n // 2, lambda j: late(j, h))
            around(p, lambda other: latest(other, h))
            span(0, g, lambda j: copy_to(0, h, 1, j, *out_way))
            span(g + 1, n, lambda j: across(j, h))
            keep(0, h, 0, *out_way)
            keep(0, h, 1, *out_way)

    def build_edge():
        for load in loads[5:7]:
            load.wait()
        loads[9].wait()
        for i, part in enumerate(column(edge_ref)):
            div_col[i * LANES : (i + 1) * LANES, :] = part
        for i in range(rows // LANES):
            at = slice(i * LANES, (i + 1) * LANES)
            inc_t[:, at] = inc[at, :].astype(F32).T.astype(BF16)
        for i in range(flat // LANES):
            at = slice(i * LANES, (i + 1) * LANES)
            row = (iota((LANES, LANES), 0) % width).astype(F32)
            target = slot_col(i * (LANES // width), LANES, in_ref) * float(width) + row
            target_t = target.T
            for k in range(edges // LANES):
                e = slice(k * LANES, (k + 1) * LANES)
                lane = (iota((LANES, LANES), 1) + k * LANES).astype(F32)
                choose_t[at, e] = jnp.where(target == lane, 1.0, 0.0).astype(BF16)
                down = (iota((LANES, LANES), 0) + k * LANES).astype(F32)
                choose[e, at] = jnp.where(target_t == down, 1.0, 0.0).astype(BF16)

    def build_node():
        for load in loads[7:9]:
            load.wait()
        known, class_of = column(mask_ref), column(seed_ref)
        for i in range(rows // LANES):
            seed_col[i * LANES : (i + 1) * LANES, :] = jnp.where(known[i] == 1.0, class_of[i], -1.0)
        for i in range(flat // LANES):
            at = slice(i * LANES, (i + 1) * LANES)
            weight, place = tile_col[at, :].T, block_col[at, :].T
            down_block = (iota((LANES, LANES), 0) // block).astype(F32)
            for k in range(rows // LANES):
                b = slice(k * LANES, (k + 1) * LANES)
                spread[b, at] = jnp.where(place == down_block + float(k * fold), weight, 0.0).astype(BF16)

    near, far = slice(0, half), slice(half, flat)

    for r in range(ROUNDS):
        if r > 0:
            with jax.named_scope("out_send"):
                out_product(r, 0)
                send_all(r, 0, 0, *out_way)
                out_product(r, 1)
                send_all(r, 0, 1, *out_way)
                for h in range(1, PARTS):
                    send_all(r, h, 0, *out_way)
                    send_all(r, h, 1, *out_way)
        else:
            with jax.named_scope("build_edge"):
                build_edge()

        with jax.named_scope("local_edge"):

            def local_edge(i):
                at = rows_of(i, 256)
                edge_sum[at, :] = dot(inc_t[at, :], scaled[...])

            loop(edges // 256, local_edge)

        for h in range(PARTS):
            part = slice(h * cols, (h + 1) * cols)
            with jax.named_scope("edge"):
                arrive(r, h, 1, frecv, frecv_sem)
                edge_sum[:, part] += dot(choose[:, far], frecv[r, h, far, :])
                arrive(r, h, 0, frecv, frecv_sem)
                for i in range(edges // 256):
                    at = slice(i * 256, (i + 1) * 256)
                    total = edge_sum[at, part] + dot(choose[at, near], frecv[r, h, near, :])
                    agg[at, part] = (total / tiled(div_col[at, :], cols // LANES)).astype(BF16)
            with jax.named_scope("back_send"):
                for kind in range(2):
                    at = slice(kind * half, (kind + 1) * half)
                    bsend[r, h, at, :] = dot(choose_t[at, :], agg[:, part]).astype(BF16)
                    send_all(r, h, kind, *back_way)
                if r == 0 and h == PARTS - 1:
                    build_node()
            with jax.named_scope("local_node"):

                def local_node(i):
                    at = rows_of(i, 256)
                    node_sum[at, part] = dot(inc[at, :], agg[:, part])

                loop(rows // 256, local_node)

        for h in range(PARTS):
            part = slice(h * cols, (h + 1) * cols)
            with jax.named_scope("node"):
                arrive(r, h, 1, brecv, brecv_sem)

                def across_node(i):
                    at = rows_of(i, 256)
                    node_sum[at, part] += dot(spread[at, far], brecv[r, h, far, :])

                loop(rows // 256, across_node)
                arrive(r, h, 0, brecv, brecv_sem)
                if h < PARTS - 1:

                    def peer_node(i):
                        at = rows_of(i, 256)
                        node_sum[at, part] += dot(spread[at, near], brecv[r, h, near, :])

                    loop(rows // 256, peer_node)

        with jax.named_scope("finish"):
            for i in range(rows // LANES):
                at = slice(i * LANES, (i + 1) * LANES)
                last = dot(spread[at, near], brecv[r, PARTS - 1, near, :])
                total = node_sum[at, :]
                if PARTS > 1:
                    total = jnp.concatenate([total[:, : classes - cols], total[:, classes - cols :] + last], axis=1)
                else:
                    total = total + last
                mean_square = jnp.sum(total * total, axis=-1, keepdims=True) * (1.0 / classes)
                normed = total * lax.rsqrt(mean_square + EPS)
                known = tiled(seed_col[at, :], classes // LANES)
                seeds = jnp.where(iota((LANES, classes), 1).astype(F32) == known, float(classes) ** 0.5, 0.0)
                current = jnp.where(known >= 0.0, seeds, normed).astype(BF16)
                if r < ROUNDS - 1:
                    scaled[at, :] = (current.astype(F32) * tiled(scale_col[at, :], classes // LANES)).astype(BF16)
                else:
                    out_ref[at, :] = current

    with jax.named_scope("sent"):
        for r in range(ROUNDS):
            for h in range(PARTS):
                for buf, sem in ((fsend, fsend_sem), (bsend, bsend_sem)):
                    sent = buf.at[r, h, pl.ds(0, (slots - 2) * width)]
                    pltpu.make_async_copy(sent, sent, sem.at[r, h]).wait()


def local(labels, node_degree, edge_degree, labeled_mask, seed_labels, local_incidence, tiles, out_block, out_count, in_edge):
    n = lax.axis_size("peer")
    rows, classes = labels.shape
    edges = local_incidence.shape[1]
    _, slots, block, width = tiles.shape
    flat = slots * width
    sizes = (n, slots, block, width, rows, edges, classes)
    travel = (ROUNDS, PARTS, flat, classes // PARTS)
    hbm = pl.BlockSpec(memory_space=pltpu.HBM)
    dma = pltpu.SemaphoreType.DMA
    args = (
        labels,
        tiles[0].transpose(1, 2, 0).reshape(block * width, slots),
        local_incidence,
        node_degree.reshape(rows // LANES, LANES),
        edge_degree.reshape(edges // LANES, LANES),
        labeled_mask.reshape(rows // LANES, LANES),
        seed_labels.reshape(rows // LANES, LANES),
        out_block,
        out_count,
        in_edge,
    )
    return pl.pallas_call(
        functools.partial(kernel, sizes),
        out_shape=pltpu.VMEM((rows, classes), BF16),
        in_specs=[hbm] * len(args),
        out_specs=pl.BlockSpec(memory_space=pltpu.VMEM),
        scratch_shapes=[pltpu.VMEM(a.shape, a.dtype) for a in args]
        + [
            pltpu.VMEM((edges, rows), BF16),
            pltpu.VMEM((rows, flat), BF16),
            pltpu.VMEM((flat, rows), BF16),
            pltpu.VMEM((edges, flat), BF16),
            pltpu.VMEM((flat, edges), BF16),
            pltpu.VMEM((flat, LANES), F32),
            pltpu.VMEM((flat, LANES), F32),
            pltpu.VMEM((rows, LANES), F32),
            pltpu.VMEM((rows, LANES), F32),
            pltpu.VMEM((edges, LANES), F32),
            pltpu.VMEM((rows, classes), BF16),
            pltpu.VMEM((edges, classes), BF16),
            pltpu.VMEM((edges, classes), F32),
            pltpu.VMEM((rows, classes), F32),
            pltpu.VMEM(travel, BF16),
            pltpu.VMEM(travel, BF16),
            pltpu.VMEM(travel, BF16),
            pltpu.VMEM(travel, BF16),
            dma((len(args),)),
            pltpu.SemaphoreType.REGULAR((slots,)),
            dma((ROUNDS, PARTS)),
            dma((ROUNDS, PARTS, 2)),
            dma((ROUNDS, PARTS)),
            dma((ROUNDS, PARTS, 2)),
        ],
        compiler_params=pltpu.CompilerParams(collective_id=0, has_side_effects=True, vmem_limit_bytes=56 << 20),
    )(*args)


def solution(mesh):
    split = ("grp", "peer")
    specs = (
        P(split, None),
        P(split),
        P(split),
        P(split),
        P(split),
        P(split, None),
        P(split, None, None, None),
        P(split, None),
        P(split, None),
        P(split, None),
    )
    return jax.shard_map(local, mesh=mesh, in_specs=specs, out_specs=P(split, None), check_vma=False)
```
